32 devices in a mesh: row: 4 (over y, core), col: 8 (over z, x).
Axes of the slice: x: 2, y: 2, z: 4, core: 2. Of those that a mesh axis runs over, the one named last changes fastest.
Arguments:
- child_vectors: bfloat16 [2, 2048, 16384], P(None, 'row', 'col'), may hold values from -6 to 6
- merge_position: int32 [2, 16384], P(None, 'col'), may hold values from 0 to 32767, as said below
- pole_frac: float32 [2, 16384], P(None, 'col'), may hold values from 0 to 0.3
- weights: float32 [2, 16384], P(None, 'col'), may hold values from -3 to 3, as said below
- retained: int32 [2, 16384], P(None, 'col'), may hold values from 0 to 1, as said below
- root_index: int32 [512], replicated, may hold values from 0 to 32766
- root_offset: float32 [512], replicated, may hold values from 0.55 to 0.75
Outputs:
- merged: bfloat16 [2, 2048, 512], P(None, ('row', 'col'))
The draws below stay inside these ranges and needn't reach their ends.
Inputs may be any that keep to these rules, and one draw needn't show every extreme that they name: `merge_position`: each merged position 0 to 32767 occurs exactly once over both children. The first pole of each aligned block of 2048 poles of a child is retained; elsewhere whole aligned blocks of 512 poles may be deflated. `weights`: magnitudes lie between 0.3 and 3.
All inputs are finite; a program needn't handle non-finite values.
Results may differ from the reference program's by a relative error of at most 0.015.
Values may be sent and summed in bfloat16 or wider, within the bound.
No kernel may reach another device: no remote copies, remote signals or barrier semaphores. Data moves between devices by JAX's collectives and lax.ppermute only.
A program may use at most 64 MiB of HBM per device.

```python
import math
import jax
import jax.numpy as jnp
from jax import lax

HALF_DEV = 2048
TILE = 512
HALF = 16384
ORDER = 32768
ROWS = 2048
COLS = 512
N_COL = 8


def draw_merge_position(key, part):
    order_values = jax.random.permutation(jax.random.fold_in(key, 11), jnp.arange(ORDER, dtype=jnp.int32))
    return order_values.reshape(2, HALF).astype(jnp.int32)


def draw_weights(key, part):
    sign_key = jax.random.fold_in(key, 21)
    size_key = jax.random.fold_in(key, 22)
    signs = jnp.where(jax.random.bernoulli(sign_key, 0.5, (2, HALF)), 1.0, -1.0)
    magnitude = jnp.exp(jax.random.uniform(size_key, (2, HALF), jnp.float32, math.log(0.3), math.log(3.0)))
    return (signs * magnitude).astype(jnp.float32)


def draw_retained(key, part):
    levels = jax.random.randint(jax.random.fold_in(key, 31), (2, HALF // TILE), 0, 5)
    coins = jax.random.randint(jax.random.fold_in(key, 32), (2, HALF), 0, 4)
    thresholds = jnp.repeat(levels, TILE, axis=1)
    leading = (jnp.arange(HALF) % HALF_DEV == 0)[None, :]
    return jnp.logical_or(coins < thresholds, leading).astype(jnp.int32)


def with_ends(result, own_key, smallest, top_value):
    longest = result.shape.index(max(result.shape))
    spots = []
    for shift in (0, 1):
        where = [jax.random.randint(jax.random.fold_in(own_key, axis), (), 0, length) for axis, length in enumerate(result.shape)]
        where[longest] = (where[longest] + shift) % result.shape[longest]
        spots.append(tuple(where))
    return result.at[spots[0]].set(smallest).at[spots[1]].set(top_value)


def block_scale(stream_key, shape, cuts, smallest, high):
    def one(position, blocks):
        draws = jax.random.uniform(jax.random.fold_in(jax.random.fold_in(stream_key, 6), position), (blocks,), jnp.float32, smallest / len(cuts), high / len(cuts))
        return jnp.repeat(jnp.exp(draws), shape[position] // blocks).reshape((-1,) + (1,) * (len(shape) - position - 1))

    gain = one(*cuts[0])
    for cut in cuts[1:]:
        gain = gain * one(*cut)
    return gain


def normal_values(stream_key, extent, scale, most, cuts=(), held_as=jnp.bfloat16):
    entries = jax.random.normal(stream_key, extent, jnp.float32) * scale
    if len(cuts) > 0:
        entries = block_scale(stream_key, extent, cuts, -0.22, 0.18) * entries
    return jnp.clip(entries, min=-most, max=most).astype(held_as)


def setup_inputs(seed: int = 0) -> dict:
    seeds = jax.random.split(jax.random.key(seed), 8)
    return {
        "child_vectors": normal_values(seeds[0], (2, ROWS, HALF), 1.0, 6.0, ((1, 4), (2, 8))),
        "merge_position": draw_merge_position(jax.random.fold_in(seeds[7], 71), 0),
        "pole_frac": jnp.clip(0.3 * jax.random.uniform(seeds[2], (2, HALF), jnp.float32) ** block_scale(seeds[2], (2, HALF), ((1, 8),), -0.2, 0.2), 0.0, 0.3),
        "weights": draw_weights(jax.random.fold_in(seeds[7], 71), 0),
        "retained": draw_retained(jax.random.fold_in(seeds[7], 71), 0),
        "root_index": with_ends(jax.random.randint(seeds[5], (COLS,), 0, ORDER - 1), jax.random.fold_in(seeds[5], 1), 0, (ORDER - 1) - 1).astype(jnp.int32),
        "root_offset": jnp.clip(jax.random.uniform(seeds[6], (COLS,), jnp.float32, 0.55, 0.75), 0.55, 0.75),
    }


def reference(child_vectors, merge_position, pole_frac, weights, retained, root_index, root_offset):
    spacing = (merge_position[:, :, None] - root_index[None, None, :]).astype(jnp.float32) + (pole_frac[:, :, None] - root_offset[None, None, :])
    raw_panel = (retained.astype(jnp.float32) * weights)[:, :, None] / spacing
    totals = lax.optimization_barrier(jnp.sum(raw_panel * raw_panel, axis=(0, 1)))
    panel_block = (raw_panel * lax.rsqrt(totals)[None, None, :]).astype(jnp.bfloat16)

    def add_block(running, number):
        first_col = (number * HALF_DEV).astype(jnp.int32)
        vector_block = lax.dynamic_slice_in_dim(child_vectors, first_col, HALF_DEV, 2).astype(jnp.float32)
        panel_part = lax.dynamic_slice_in_dim(panel_block, first_col, HALF_DEV, 1).astype(jnp.float32)
        partial_value = jnp.einsum('crh,chm->crm', vector_block, panel_part)
        rounded = lax.optimization_barrier(partial_value.astype(jnp.bfloat16)).astype(jnp.float32)
        return (running + rounded, None)
    running, unused = lax.scan(add_block, jnp.zeros((2, ROWS, COLS), jnp.float32), jnp.arange(N_COL, dtype=jnp.int32))
    return running.astype(jnp.bfloat16)
```

```python
import functools

import jax
import jax.numpy as jnp
from jax import lax
from jax.experimental import pallas as pl
from jax.experimental.pallas import tpu as pltpu
from jax.sharding import PartitionSpec as P

LANES = 128
VMEM = pl.BlockSpec(memory_space=pltpu.VMEM)
F32, BF16 = jnp.float32, jnp.bfloat16


def radices(n):
    near = min(4, n)
    return near, n // near


def child_kernel(child, near, far, *refs):
    pos_ref, frac_ref, weight_ref, kept_ref, root_ref, off_ref, vec_ref = refs[:7]
    outs = refs[7 : 7 + near]
    total_ref = refs[7 + near]
    vec, panel, poles, roots, sums, sems = refs[8 + near :]
    rows, depth = vec.shape
    cols = panel.shape[0]
    block = rows // (near * far)
    me = lax.rem(lax.axis_index("col"), near)

    copies = []
    for k in range(near):
        target = jnp.bitwise_xor(me, k)
        for h in range(far):
            first = pl.multiple_of((h * near + target) * block, block)
            copy = pltpu.make_async_copy(
                vec_ref.at[child, pl.ds(first, block), :],
                vec.at[pl.ds((k * far + h) * block, block), :],
                sems.at[k, h],
            )
            copy.start()
            copies.append(copy)

    own = pl.ds(child, 1)
    for number, row in enumerate(
        (
            pos_ref[own, :].astype(F32),
            frac_ref[own, :],
            kept_ref[own, :].astype(F32) * weight_ref[own, :],
        )
    ):
        poles[number] = jnp.broadcast_to(row, (8, depth))
    for first in range(0, cols, LANES):
        for number, ref in enumerate((root_ref, off_ref)):
            row = ref[:, first : first + LANES].astype(F32)
            roots[number, first : first + LANES, :] = jnp.broadcast_to(row, (LANES, LANES)).T

    def columns(step, carry):
        at = pl.ds(pl.multiple_of(step * 16, 16), 16)
        root = roots[0, at, :].reshape(2, 8, LANES)
        off = roots[1, at, :].reshape(2, 8, LANES)
        total = jnp.zeros((2, 8, LANES), F32)
        for first in range(0, depth, LANES):
            here = slice(first, first + LANES)
            spacing = (poles[0, :, here] - root) + (poles[1, :, here] - off)
            inverse = pl.reciprocal(spacing, approx=True)
            inverse = inverse * (2.0 - spacing * inverse)
            raw = poles[2, :, here] * inverse
            total = total + raw * raw
            panel[at, here] = raw.reshape(16, LANES).astype(BF16)
        sums[at, :] = total.reshape(16, LANES)
        return carry

    lax.fori_loop(0, cols // 16, columns, 0)
    for first in range(0, cols, LANES):
        here = slice(first, first + LANES)
        total_ref[:, here] = jnp.sum(sums[here, :].T, axis=0, keepdims=True)
    for copy in copies:
        copy.wait()
    width = min(256, cols)
    for first in range(0, cols, width):
        here = slice(first, first + width)
        part = lax.dot_general(
            vec[...], panel[here, :], (((1,), (1,)), ((), ())), preferred_element_type=F32
        ).astype(BF16)
        for k in range(near):
            outs[k][:, here] = part[k * far * block : (k + 1) * far * block]


def child_call(child, near, far, poles, roots, vectors):
    rows, depth = vectors.shape[1:]
    cols = roots[0].shape[1]
    return pl.pallas_call(
        functools.partial(child_kernel, child, near, far),
        out_shape=[jax.ShapeDtypeStruct((rows // near, cols), BF16)] * near
        + [jax.ShapeDtypeStruct((1, cols), F32)],
        in_specs=[VMEM] * 6 + [pl.BlockSpec(memory_space=pl.ANY)],
        out_specs=[VMEM] * (near + 1),
        scratch_shapes=[
            pltpu.VMEM((rows, depth), BF16),
            pltpu.VMEM((cols, depth), BF16),
            pltpu.VMEM((3, 8, depth), F32),
            pltpu.VMEM((2, cols, LANES), F32),
            pltpu.VMEM((cols, LANES), F32),
            pltpu.SemaphoreType.DMA((near, far)),
        ],
        compiler_params=pltpu.CompilerParams(vmem_limit_bytes=24 * 2**20),
        cost_estimate=pl.CostEstimate(
            flops=2 * rows * depth * cols, bytes_accessed=2 * rows * depth, transcendentals=depth * cols
        ),
    )(*poles, *roots, vectors)


def middle_kernel(near, far, *refs):
    parts, totals, (own_ref, *outs), total_ref = (
        refs[:near],
        refs[near : 2 * near],
        refs[2 * near : 2 * near + far],
        refs[2 * near + far],
    )
    block = own_ref.shape[0]
    me = lax.div(lax.axis_index("col"), near)
    for k in range(far):
        at = pl.ds(pl.multiple_of(jnp.bitwise_xor(me, k) * block, block), block)
        value = parts[0][at, :].astype(F32)
        for part in parts[1:]:
            value = value + part[at, :].astype(F32)
        if k:
            outs[k - 1][...] = value.astype(BF16)
        else:
            own_ref[...] = value
    total = totals[0][...]
    for part in totals[1:]:
        total = total + part[...]
    total_ref[...] = total


def middle_call(near, far, parts, totals):
    rows, cols = parts[0].shape
    shape = (rows // far, cols)
    return pl.pallas_call(
        functools.partial(middle_kernel, near, far),
        out_shape=[jax.ShapeDtypeStruct(shape, F32)]
        + [jax.ShapeDtypeStruct(shape, BF16)] * (far - 1)
        + [jax.ShapeDtypeStruct((1, cols), F32)],
        in_specs=[VMEM] * (2 * near),
        out_specs=[VMEM] * (far + 1),
    )(*parts, *totals)


def last_kernel(children, far, *refs):
    out_ref = refs[-1]
    per = 2 * far
    total = None
    for child in range(children):
        for ref in refs[child * per + far : (child + 1) * per]:
            total = ref[...] if total is None else total + ref[...]
    scale = lax.rsqrt(total)
    for child in range(children):
        value = refs[child * per][...]
        for ref in refs[child * per + 1 : child * per + far]:
            value = value + ref[...].astype(F32)
        out_ref[child] = (value * scale).astype(BF16)


def exchange(parts, stride, n):
    return [parts[0]] + [
        lax.ppermute(part, "col", [(i, i ^ (k * stride)) for i in range(n)])
        for k, part in enumerate(parts)
        if k
    ]


def solution(mesh):
    n = mesh.shape["col"]
    near, far = radices(n)

    def local(vectors, position, fraction, weight, retained, root_index, root_offset):
        children = vectors.shape[0]
        roots = (root_index[None, :], root_offset[None, :])
        ends = []
        for child in range(children):
            *parts, total = child_call(
                child, near, far, (position, fraction, weight, retained), roots, vectors
            )
            parts = exchange(parts, 1, n)
            totals = exchange([total] * near, 1, n)
            *parts, total = middle_call(near, far, parts, totals)
            parts = exchange(parts, near, n)
            totals = exchange([total] * far, near, n)
            ends += parts + totals
        block, cols = ends[0].shape
        return pl.pallas_call(
            functools.partial(last_kernel, children, far),
            out_shape=jax.ShapeDtypeStruct((children, block, cols), BF16),
            in_specs=[VMEM] * len(ends),
            out_specs=VMEM,
        )(*ends)

    return jax.shard_map(
        local,
        mesh=mesh,
        in_specs=(P(None, "row", "col"),) + (P(None, "col"),) * 4 + (P(), P()),
        out_specs=P(None, ("row", "col"), None),
        check_vma=False,
    )
```

```python
import functools

import jax
import jax.numpy as jnp
from jax import lax
from jax.experimental import pallas as pl
from jax.experimental.pallas import tpu as pltpu
from jax.sharding import PartitionSpec as P

LANES = 128
VMEM = pl.BlockSpec(memory_space=pltpu.VMEM)
ANY = pl.BlockSpec(memory_space=pl.ANY)
F32, BF16 = jnp.float32, jnp.bfloat16
SMALL = pltpu.CompilerParams(vmem_limit_bytes=6 * 2**20)


def radices(n):
    near = min(4, n)
    return near, n // near


def tail_rows(tiles):
    return -(-3 * tiles // 16) * 16


def write_tail(total, ref, first):
    tiles = total.shape[0]
    high = total.astype(BF16).astype(F32)
    rest = total - high
    middle = rest.astype(BF16).astype(F32)
    pieces = [high, middle, rest - middle]
    spare = tail_rows(tiles) - 3 * tiles
    if spare:
        pieces.append(jnp.zeros((spare, LANES), F32))
    ref[first:, :] = jnp.concatenate(pieces, axis=0).astype(BF16)


def read_tail(ref, tiles):
    tail = ref[ref.shape[0] - tail_rows(tiles) :, :].astype(F32)
    return (tail[2 * tiles : 3 * tiles] + tail[tiles : 2 * tiles]) + tail[:tiles]


def child_kernel(child, near, far, *refs):
    pole_refs, root_refs, vec_ref = refs[:4], refs[4:6], refs[6]
    outs = refs[7 : 7 + near]
    vec, panels, poles, pole_in, kept_in, root_in, index_in, roots, sums, staged, sems, in_sems, out_sems = refs[7 + near :]
    rows, depth = vec.shape
    width = panels.shape[1]
    cols = roots.shape[1]
    tiles = cols // LANES
    part = rows // near
    block = part // far
    me = lax.rem(lax.axis_index("col"), near)

    pos_ref, frac_ref, weight_ref, kept_ref = pole_refs
    small = [
        pltpu.make_async_copy(source, target, in_sems.at[number])
        for number, (source, target) in enumerate(
            (
                (root_refs[0], index_in),
                (root_refs[1], root_in),
                (pos_ref, kept_in.at[0]),
                (frac_ref, pole_in.at[0]),
                (weight_ref, pole_in.at[1]),
                (kept_ref, kept_in.at[1]),
            )
        )
    ]
    for copy in small:
        copy.start()
    large = []
    for k in range(near):
        target = jnp.bitwise_xor(me, k)
        for h in range(far):
            first = pl.multiple_of((h * near + target) * block, block)
            large.append(
                pltpu.make_async_copy(
                    vec_ref.at[child, pl.ds(first, block), :],
                    vec.at[pl.ds(k * part + h * block, block), :],
                    sems.at[k, h],
                )
            )
    for copy in large:
        copy.start()
    for copy in small:
        copy.wait()

    for first in range(0, cols, LANES):
        for number, row in enumerate((index_in[:, first : first + LANES].astype(F32), root_in[:, first : first + LANES])):
            roots[number, first : first + LANES, :] = jnp.broadcast_to(row, (LANES, LANES)).T
    own = slice(child, child + 1)
    for number, row in enumerate(
        (
            kept_in[0, own, :].astype(F32),
            pole_in[0, own, :],
            kept_in[1, own, :].astype(F32) * pole_in[1, own, :],
        )
    ):
        poles[number] = jnp.broadcast_to(row, (8, depth))

    def form(first_col, panel):
        for row in range(0, width, 16):
            at = slice(first_col + row, first_col + row + 16)
            root = roots[0, at, :].reshape(2, 8, LANES)
            off = roots[1, at, :].reshape(2, 8, LANES)
            total = jnp.zeros((2, 8, LANES), F32)
            for first in range(0, depth, LANES):
                here = slice(first, first + LANES)
                spacing = (poles[0, :, here] - root) + (poles[1, :, here] - off)
                inverse = pl.reciprocal(spacing, approx=True)
                inverse = inverse * (2.0 - spacing * inverse)
                raw = poles[2, :, here] * inverse
                total = total + raw * raw
                panel[row : row + 16, here] = raw.reshape(16, LANES).astype(BF16)
            sums[at, :] = total.reshape(16, LANES)

    def send(first_col, panel):
        value = lax.dot_general(
            vec[...], panel[...], (((1,), (1,)), ((), ())), preferred_element_type=F32
        ).astype(BF16)
        for k in range(near):
            for first in range(0, width, LANES):
                tile = (first_col + first) // LANES
                staged[k, tile * part : (tile + 1) * part, :] = value[
                    k * part : (k + 1) * part, first : first + LANES
                ]

    firsts = list(range(0, cols, width))
    form(firsts[0], panels.at[0])
    for copy in large:
        copy.wait()
    for number, first in enumerate(firsts):
        if number + 1 < len(firsts):
            form(firsts[number + 1], panels.at[(number + 1) % 2])
        else:
            total = jnp.concatenate(
                [
                    jnp.sum(sums[at : at + LANES, :].T, axis=0, keepdims=True)
                    for at in range(0, cols, LANES)
                ],
                axis=0,
            )
            for k in range(near):
                write_tail(total, staged.at[k], tiles * part)
        send(first, panels.at[number % 2])
    copies = [pltpu.make_async_copy(staged.at[k], outs[k], out_sems.at[k]) for k in range(near)]
    for copy in copies:
        copy.start()
    for copy in copies:
        copy.wait()


def child_call(child, near, far, poles, roots, vectors):
    children, rows, depth = vectors.shape
    cols = roots[0].shape[1]
    tiles = cols // LANES
    width = min(256, cols)
    shape = (tiles * (rows // near) + tail_rows(tiles), LANES)
    return pl.pallas_call(
        functools.partial(child_kernel, child, near, far),
        out_shape=[jax.ShapeDtypeStruct(shape, BF16)] * near,
        in_specs=[ANY] * 7,
        out_specs=[ANY] * near,
        scratch_shapes=[
            pltpu.VMEM((rows, depth), BF16),
            pltpu.VMEM((2, width, depth), BF16),
            pltpu.VMEM((3, 8, depth), F32),
            pltpu.VMEM((2, children, depth), F32),
            pltpu.VMEM((2, children, depth), jnp.int32),
            pltpu.VMEM((1, cols), F32),
            pltpu.VMEM((1, cols), jnp.int32),
            pltpu.VMEM((2, cols, LANES), F32),
            pltpu.VMEM((cols, LANES), F32),
            pltpu.VMEM((near, *shape), BF16),
            pltpu.SemaphoreType.DMA((near, far)),
            pltpu.SemaphoreType.DMA((6,)),
            pltpu.SemaphoreType.DMA((near,)),
        ],
        compiler_params=pltpu.CompilerParams(vmem_limit_bytes=60 * 2**20),
        cost_estimate=pl.CostEstimate(
            flops=2 * rows * depth * cols, bytes_accessed=2 * rows * depth, transcendentals=depth * cols
        ),
    )(*poles, *roots, vectors)


def middle_kernel(far, tiles, *refs):
    parts, (own_ref, total_ref, *outs) = refs[: -1 - far], refs[-1 - far :]
    block = own_ref.shape[0] // tiles
    me = lax.div(lax.axis_index("col"), len(parts))
    total = read_tail(parts[0], tiles)
    for part in parts[1:]:
        total = total + read_tail(part, tiles)
    total_ref[...] = total
    for out in outs:
        write_tail(total, out, tiles * block)
    for k in range(far):
        target = jnp.bitwise_xor(me, k)
        for tile in range(tiles):
            at = pl.ds(pl.multiple_of((tile * far + target) * block, block), block)
            value = parts[0][at, :].astype(F32)
            for part in parts[1:]:
                value = value + part[at, :].astype(F32)
            here = slice(tile * block, (tile + 1) * block)
            if k:
                outs[k - 1][here, :] = value.astype(BF16)
            else:
                own_ref[here, :] = value


def middle_call(far, tiles, parts):
    rows = (parts[0].shape[0] - tail_rows(tiles)) // far
    return pl.pallas_call(
        functools.partial(middle_kernel, far, tiles),
        out_shape=[
            jax.ShapeDtypeStruct((rows, LANES), F32),
            jax.ShapeDtypeStruct((tiles, LANES), F32),
        ]
        + [jax.ShapeDtypeStruct((rows + tail_rows(tiles), LANES), BF16)] * (far - 1),
        in_specs=[VMEM] * len(parts),
        out_specs=[VMEM] * (far + 1),
        compiler_params=SMALL,
    )(*parts)


def last_kernel(children, far, *refs):
    out_ref = refs[-1]
    tiles = out_ref.shape[2] // LANES
    block = out_ref.shape[1]
    groups = [refs[child * (far + 1) : (child + 1) * (far + 1)] for child in range(children)]
    total = None
    for _, own_total, *parts in groups:
        for value in [own_total[...]] + [read_tail(part, tiles) for part in parts]:
            total = value if total is None else total + value
    scale = lax.rsqrt(total)
    for child, (own, _, *parts) in enumerate(groups):
        for tile in range(tiles):
            here = slice(tile * block, (tile + 1) * block)
            value = own[here, :]
            for part in parts:
                value = value + part[here, :].astype(F32)
            out_ref[child, :, tile * LANES : (tile + 1) * LANES] = (
                value * scale[tile : tile + 1, :]
            ).astype(BF16)


def exchange(parts, stride, n):
    return [parts[0]] + [
        lax.ppermute(part, "col", [(i, i ^ (k * stride)) for i in range(n)])
        for k, part in enumerate(parts)
        if k
    ]


def solution(mesh):
    n = mesh.shape["col"]
    near, far = radices(n)

    def local(vectors, position, fraction, weight, retained, root_index, root_offset):
        children, rows, _ = vectors.shape
        cols = root_index.shape[0]
        tiles = cols // LANES
        roots = (root_index[None, :], root_offset[None, :])
        poles = (position, fraction, weight, retained)
        ends = []
        for child in range(children):
            parts = exchange(child_call(child, near, far, poles, roots, vectors), 1, n)
            own, total, *parts = middle_call(far, tiles, parts)
            ends += [own, total] + exchange([own] + parts, near, n)[1:]
        return pl.pallas_call(
            functools.partial(last_kernel, children, far),
            out_shape=jax.ShapeDtypeStruct((children, rows // n, cols), BF16),
            in_specs=[VMEM] * len(ends),
            out_specs=VMEM,
            compiler_params=SMALL,
        )(*ends)

    return jax.shard_map(
        local,
        mesh=mesh,
        in_specs=(P(None, "row", "col"),) + (P(None, "col"),) * 4 + (P(), P()),
        out_specs=P(None, ("row", "col"), None),
        check_vma=False,
    )
```

```python
import functools

import jax
import jax.numpy as jnp
from jax import lax
from jax.experimental import pallas as pl
from jax.experimental.pallas import tpu as pltpu
from jax.sharding import PartitionSpec as P

LANES = 128
VMEM = pl.BlockSpec(memory_space=pltpu.VMEM)
ANY = pl.BlockSpec(memory_space=pl.ANY)
F32, BF16 = jnp.float32, jnp.bfloat16
SMALL = pltpu.CompilerParams(vmem_limit_bytes=6 * 2**20)
LARGE = pltpu.CompilerParams(vmem_limit_bytes=24 * 2**20)


def radices(n):
    near = min(4, max(1, n // 2))
    return near, n // near


def tail_rows(tiles):
    return -(-3 * tiles // 16) * 16


def write_tail(total, ref):
    tiles = total.shape[0]
    high = total.astype(BF16).astype(F32)
    rest = total - high
    middle = rest.astype(BF16).astype(F32)
    pieces = [high, middle, rest - middle]
    spare = tail_rows(tiles) - 3 * tiles
    if spare:
        pieces.append(jnp.zeros((spare, LANES), F32))
    ref[ref.shape[0] - tail_rows(tiles) :, :] = jnp.concatenate(pieces, axis=0).astype(BF16)


def read_tail(ref, tiles):
    tail = ref[ref.shape[0] - tail_rows(tiles) :, :].astype(F32)
    return (tail[2 * tiles : 3 * tiles] + tail[tiles : 2 * tiles]) + tail[:tiles]


def multiply(vec, panel, first_tile, near, groups, outs):
    block = vec.shape[0] // (near * groups)
    me = lax.rem(lax.axis_index("col"), near)
    order = [(group, k) for group in range(groups) for k in range(near)]
    left = jnp.concatenate(
        [
            vec[pl.ds(pl.multiple_of((group * near + jnp.bitwise_xor(me, k)) * block, block), block), :]
            for group, k in order
        ],
        axis=0,
    )
    value = lax.dot_general(
        left, panel[...], (((1,), (1,)), ((), ())), preferred_element_type=F32
    ).astype(BF16)
    for place, (group, k) in enumerate(order):
        for tile in range(value.shape[1] // LANES):
            target = ((first_tile + tile) * groups + group) * block
            outs[k][target : target + block, :] = value[
                place * block : (place + 1) * block, tile * LANES : (tile + 1) * LANES
            ]


def away_kernel(near, far, width, *refs):
    pos_ref, frac_ref, weight_ref, kept_ref, root_ref, off_ref, vec_ref = refs[:7]
    outs = refs[7 : 7 + near]
    own_vec, panels, vec, poles, pole_in, kept_in, root_in, index_in, roots, sums, sems, in_sems = refs[7 + near :]
    children, cols, depth = panels.shape
    tiles = cols // LANES
    chunk = own_vec.shape[1]
    me = lax.div(lax.axis_index("col"), near)

    small = [
        pltpu.make_async_copy(source, target, in_sems.at[number])
        for number, (source, target) in enumerate(
            (
                (root_ref, index_in),
                (off_ref, root_in),
                (pos_ref, kept_in.at[0]),
                (frac_ref, pole_in.at[0]),
                (weight_ref, pole_in.at[1]),
                (kept_ref, kept_in.at[1]),
            )
        )
    ]
    large = [
        [
            pltpu.make_async_copy(
                vec_ref.at[child, pl.ds(pl.multiple_of(jnp.bitwise_xor(me, j) * chunk, chunk), chunk), :],
                vec.at[child, pl.ds((j - 1) * chunk, chunk), :] if j else own_vec.at[child],
                sems.at[child, j],
            )
            for j in range(far)
        ]
        for child in range(children)
    ]
    for copy in small:
        copy.start()
    for copies in large:
        for copy in copies[1:]:
            copy.start()
    for copy in small:
        copy.wait()
    for copies in large:
        copies[0].start()

    both = jnp.concatenate([index_in[...].astype(F32), root_in[...], jnp.zeros((6, cols), F32)], axis=0).T
    for number in range(2):
        roots[number] = jnp.broadcast_to(both[:, number : number + 1], (cols, LANES))
    for child in range(children):
        own = slice(child, child + 1)
        poles[child, 0] = jnp.broadcast_to(kept_in[0, own, :].astype(F32), (8, depth))
        poles[child, 1] = jnp.broadcast_to(pole_in[0, own, :], (8, depth))
        scaled = kept_in[1, own, :].astype(F32) * pole_in[1, own, :]
        poles[child, 2] = jnp.broadcast_to(scaled, (8, depth))

    def form(child, first_col):
        for row in range(first_col, first_col + width, 16):
            at = slice(row, row + 16)
            root = roots[0, at, :].reshape(2, 8, LANES)
            off = roots[1, at, :].reshape(2, 8, LANES)
            total = sums[at, :].reshape(2, 8, LANES) if child else jnp.zeros((2, 8, LANES), F32)
            for first in range(0, depth, LANES):
                here = slice(first, first + LANES)
                spacing = (poles[child, 0, :, here] - root) + (poles[child, 1, :, here] - off)
                raw = poles[child, 2, :, here] * pl.reciprocal(spacing, approx=True)
                total = total + raw * raw
                panels[child, at, here] = raw.reshape(16, LANES).astype(BF16)
            sums[at, :] = total.reshape(16, LANES)

    units = [(child, first) for child in range(children) for first in range(0, cols, width)]
    form(*units[0])
    for number, (child, first) in enumerate(units):
        if first == 0:
            for copy in large[child][1:]:
                copy.wait()
        if number + 1 < len(units):
            form(*units[number + 1])
        else:
            total = jnp.concatenate(
                [
                    jnp.sum(sums[at : at + LANES, :].T, axis=0, keepdims=True)
                    for at in range(0, cols, LANES)
                ],
                axis=0,
            )
            for out in outs:
                write_tail(total, out)
        panel = panels.at[child, first : first + width, :]
        multiply(vec.at[child], panel, child * tiles + first // LANES, near, far - 1, outs)
    for copies in large:
        copies[0].wait()


def own_kernel(near, width, vec, panels, *outs):
    children, cols, _ = panels.shape
    for child in range(children):
        for first in range(0, cols, width):
            panel = panels.at[child, first : first + width, :]
            multiply(vec.at[child], panel, (child * cols + first) // LANES, near, 1, outs)


def child_calls(near, far, poles, roots, vectors):
    children, rows, depth = vectors.shape
    cols = roots[0].shape[1]
    width = min(256, cols)
    tiles = cols // LANES
    chunk = rows // far
    block = chunk // near
    flops = 2 * children * chunk * depth * cols
    *away, own_vec, panels = pl.pallas_call(
        functools.partial(away_kernel, near, far, width),
        out_shape=[pltpu.VMEM((children * tiles * (far - 1) * block + tail_rows(tiles), LANES), BF16)] * near
        + [pltpu.VMEM((children, chunk, depth), BF16), pltpu.VMEM((children, cols, depth), BF16)],
        in_specs=[ANY] * 7,
        out_specs=[VMEM] * (near + 2),
        scratch_shapes=[
            pltpu.VMEM((children, rows - chunk, depth), BF16),
            pltpu.VMEM((children, 3, 8, depth), F32),
            pltpu.VMEM((2, children, depth), F32),
            pltpu.VMEM((2, children, depth), jnp.int32),
            pltpu.VMEM((1, cols), F32),
            pltpu.VMEM((1, cols), jnp.int32),
            pltpu.VMEM((2, cols, LANES), F32),
            pltpu.VMEM((cols, LANES), F32),
            pltpu.SemaphoreType.DMA((children, far)),
            pltpu.SemaphoreType.DMA((6,)),
        ],
        compiler_params=LARGE,
        cost_estimate=pl.CostEstimate(
            flops=flops * (far - 1),
            bytes_accessed=2 * children * rows * depth,
            transcendentals=children * depth * cols,
        ),
    )(*(pltpu.with_memory_space_constraint(x, pltpu.HBM) for x in (*poles, *roots, vectors)))
    own = pl.pallas_call(
        functools.partial(own_kernel, near, width),
        out_shape=[pltpu.VMEM((children * tiles * block, LANES), BF16)] * near,
        in_specs=[VMEM] * 2,
        out_specs=[VMEM] * near,
        compiler_params=LARGE,
        cost_estimate=pl.CostEstimate(flops=flops, bytes_accessed=0, transcendentals=0),
    )(own_vec, panels)
    return away, own


def middle_kernel(near, tiles, block, *refs):
    parts, total_ref, outs = refs[:near], refs[near + 1], refs[near + 2 :]
    total = read_tail(parts[0], tiles)
    for part in parts[1:]:
        total = total + read_tail(part, tiles)
    total_ref[...] = total
    groups = len(outs)
    rows = outs[0].shape[0] - tail_rows(tiles)
    size = rows if groups == 1 else block
    for group, out in enumerate(outs):
        write_tail(total, out)
        for first in range(0, rows, size):
            at = slice(first * groups + group * size, first * groups + (group + 1) * size)
            value = parts[0][at, :].astype(F32)
            for part in parts[1:]:
                value = value + part[at, :].astype(F32)
            out[first : first + size, :] = value.astype(BF16)


def middle_call(near, far, tiles, block, parts, after):
    rows = (parts[0].shape[0] - tail_rows(tiles)) // (far - 1)
    return pl.pallas_call(
        functools.partial(middle_kernel, near, tiles, block),
        out_shape=[jax.ShapeDtypeStruct((tiles, LANES), F32)]
        + [jax.ShapeDtypeStruct((rows + tail_rows(tiles), LANES), BF16)] * (far - 1),
        in_specs=[VMEM] * near + [ANY],
        out_specs=[VMEM] * far,
        compiler_params=SMALL,
    )(*parts, after)


def sum_kernel(*refs):
    value = refs[0][...].astype(F32)
    for part in refs[1:-1]:
        value = value + part[...].astype(F32)
    refs[-1][...] = value


def sum_call(parts):
    return pl.pallas_call(
        sum_kernel,
        out_shape=jax.ShapeDtypeStruct(parts[0].shape, F32),
        in_specs=[VMEM] * len(parts),
        out_specs=VMEM,
        compiler_params=SMALL,
        cost_estimate=pl.CostEstimate(flops=4 * 10**10, bytes_accessed=0, transcendentals=0),
    )(*parts)


def last_kernel(*refs):
    total_ref, own, others, out_ref = refs[0], refs[1], refs[2:-1], refs[-1]
    children, block, cols = out_ref.shape
    tiles = cols // LANES
    total = total_ref[...]
    for other in others:
        total = total + read_tail(other, tiles)
    scale = lax.rsqrt(total)
    for child in range(children):
        for tile in range(tiles):
            at = slice((child * tiles + tile) * block, (child * tiles + tile + 1) * block)
            value = own[at, :]
            for part in others:
                value = value + part[at, :].astype(F32)
            out_ref[child, :, tile * LANES : (tile + 1) * LANES] = (
                value * scale[tile : tile + 1, :]
            ).astype(BF16)


def exchange(parts, stride, n):
    got = list(parts)
    for k in sorted(range(1, len(parts)), key=lambda k: (k.bit_count(), -k)):
        got[k] = lax.ppermute(parts[k], "col", [(i, i ^ (k * stride)) for i in range(n)])
    return got


def solution(mesh):
    n = mesh.shape["col"]
    near, far = radices(n)

    def local(vectors, position, fraction, weight, retained, root_index, root_offset):
        children, rows, _ = vectors.shape
        cols = root_index.shape[0]
        block = rows // n
        roots = (root_index[None, :], root_offset[None, :])
        poles = (position, fraction, weight, retained)
        away, own = child_calls(near, far, poles, roots, vectors)
        away = exchange(away, 1, n)
        total, *sums = middle_call(near, far, cols // LANES, block, away, own[0])
        own = sum_call(exchange(own, 1, n))
        others = exchange([total] + sums, near, n)[1:]
        return pl.pallas_call(
            last_kernel,
            out_shape=jax.ShapeDtypeStruct((children, block, cols), BF16),
            in_specs=[VMEM] * (2 + len(others)),
            out_specs=VMEM,
            compiler_params=SMALL,
        )(total, own, *others)

    return jax.shard_map(
        local,
        mesh=mesh,
        in_specs=(P(None, "row", "col"),) + (P(None, "col"),) * 4 + (P(), P()),
        out_specs=P(None, ("row", "col"), None),
        check_vma=False,
    )
```

```python
import functools

import jax
import jax.numpy as jnp
from jax import lax
from jax.experimental import pallas as pl
from jax.experimental.pallas import tpu as pltpu
from jax.sharding import PartitionSpec as P

LANES = 128
VMEM = pl.BlockSpec(memory_space=pltpu.VMEM)
ANY = pl.BlockSpec(memory_space=pl.ANY)
F32, BF16 = jnp.float32, jnp.bfloat16
SMALL = pltpu.CompilerParams(vmem_limit_bytes=6 * 2**20)
LARGE = pltpu.CompilerParams(vmem_limit_bytes=24 * 2**20)


def radices(n):
    near = min(4, max(1, n // 2))
    return near, n // near


def tail_rows(tiles):
    return -(-3 * tiles // 16) * 16


def write_tail(total, ref):
    tiles = total.shape[0]
    high = total.astype(BF16).astype(F32)
    rest = total - high
    middle = rest.astype(BF16).astype(F32)
    pieces = [high, middle, rest - middle]
    spare = tail_rows(tiles) - 3 * tiles
    if spare:
        pieces.append(jnp.zeros((spare, LANES), F32))
    ref[ref.shape[0] - tail_rows(tiles) :, :] = jnp.concatenate(pieces, axis=0).astype(BF16)


def read_tail(ref, tiles):
    tail = ref[ref.shape[0] - tail_rows(tiles) :, :].astype(F32)
    return (tail[2 * tiles : 3 * tiles] + tail[tiles : 2 * tiles]) + tail[:tiles]


def multiply(vec, panel, first_tile, near, groups, outs):
    block = vec.shape[0] // (near * groups)
    me = lax.rem(lax.axis_index("col"), near)
    order = [(group, k) for group in range(groups) for k in range(near)]
    left = jnp.concatenate(
        [
            vec[pl.ds(pl.multiple_of((group * near + jnp.bitwise_xor(me, k)) * block, block), block), :]
            for group, k in order
        ],
        axis=0,
    )
    value = lax.dot_general(
        left, panel[...], (((1,), (1,)), ((), ())), preferred_element_type=F32
    ).astype(BF16)
    for place, (group, k) in enumerate(order):
        for tile in range(value.shape[1] // LANES):
            target = ((first_tile + tile) * groups + group) * block
            outs[k][target : target + block, :] = value[
                place * block : (place + 1) * block, tile * LANES : (tile + 1) * LANES
            ]


def away_kernel(near, far, width, *refs):
    pos_ref, frac_ref, weight_ref, kept_ref, root_ref, off_ref, vec_ref = refs[:7]
    outs = refs[7 : 7 + near]
    own_vec, panels, vec, poles, pole_in, kept_in, root_in, index_in, roots, sums, sems, in_sems = refs[7 + near :]
    children, cols, depth = panels.shape
    tiles = cols // LANES
    chunk = own_vec.shape[1]
    me = lax.div(lax.axis_index("col"), near)

    small = [
        pltpu.make_async_copy(source, target, in_sems.at[number])
        for number, (source, target) in enumerate(
            (
                (root_ref, index_in),
                (off_ref, root_in),
                (pos_ref, kept_in.at[0]),
                (frac_ref, pole_in.at[0]),
                (weight_ref, pole_in.at[1]),
                (kept_ref, kept_in.at[1]),
            )
        )
    ]
    large = [
        [
            pltpu.make_async_copy(
                vec_ref.at[child, pl.ds(pl.multiple_of(jnp.bitwise_xor(me, j) * chunk, chunk), chunk), :],
                vec.at[child, pl.ds((j - 1) * chunk, chunk), :] if j else own_vec.at[child],
                sems.at[child, j],
            )
            for j in range(1 if child + 1 == children else 0, far)
        ]
        for child in range(children)
    ]
    for copy in small:
        copy.start()
    for copies in large:
        for copy in copies[1 - far :]:
            copy.start()
    for copy in small:
        copy.wait()
    for copies in large[:-1]:
        copies[0].start()

    both = jnp.concatenate([index_in[...].astype(F32), root_in[...], jnp.zeros((6, cols), F32)], axis=0).T
    for number in range(2):
        roots[number] = jnp.broadcast_to(both[:, number : number + 1], (cols, LANES))
    for child in range(children):
        own = slice(child, child + 1)
        poles[child, 0] = jnp.broadcast_to(kept_in[0, own, :].astype(F32), (8, depth))
        poles[child, 1] = jnp.broadcast_to(pole_in[0, own, :], (8, depth))
        scaled = kept_in[1, own, :].astype(F32) * pole_in[1, own, :]
        poles[child, 2] = jnp.broadcast_to(scaled, (8, depth))

    def form(child, first_col):
        for row in range(first_col, first_col + width, 16):
            at = slice(row, row + 16)
            root = roots[0, at, :].reshape(2, 8, LANES)
            off = roots[1, at, :].reshape(2, 8, LANES)
            total = sums[at, :].reshape(2, 8, LANES) if child else jnp.zeros((2, 8, LANES), F32)
            for first in range(0, depth, LANES):
                here = slice(first, first + LANES)
                spacing = (poles[child, 0, :, here] - root) + (poles[child, 1, :, here] - off)
                raw = poles[child, 2, :, here] * pl.reciprocal(spacing, approx=True)
                total = total + raw * raw
                panels[child, at, here] = raw.reshape(16, LANES).astype(BF16)
            sums[at, :] = total.reshape(16, LANES)

    units = [(child, first) for child in range(children) for first in range(0, cols, width)]
    form(*units[0])
    for number, (child, first) in enumerate(units):
        if first == 0:
            for copy in large[child][1 - far :]:
                copy.wait()
        if number + 1 < len(units):
            form(*units[number + 1])
        else:
            total = jnp.concatenate(
                [
                    jnp.sum(sums[at : at + LANES, :].T, axis=0, keepdims=True)
                    for at in range(0, cols, LANES)
                ],
                axis=0,
            )
            for out in outs:
                write_tail(total, out)
        panel = panels.at[child, first : first + width, :]
        multiply(vec.at[child], panel, child * tiles + first // LANES, near, far - 1, outs)
    for copies in large[:-1]:
        copies[0].wait()


def own_kernel(near, width, own_vec, panels, vec_ref, *refs):
    outs, (last_vec, sem) = refs[:near], refs[near:]
    children, cols, _ = panels.shape
    chunk = last_vec.shape[0]
    me = lax.div(lax.axis_index("col"), near)
    rows = pl.ds(pl.multiple_of(me * chunk, chunk), chunk)
    copy = pltpu.make_async_copy(vec_ref.at[children - 1, rows, :], last_vec, sem)
    copy.start()
    for child in range(children):
        vec = last_vec if child + 1 == children else own_vec.at[child]
        if child + 1 == children:
            copy.wait()
        for first in range(0, cols, width):
            panel = panels.at[child, first : first + width, :]
            multiply(vec, panel, (child * cols + first) // LANES, near, 1, outs)


def child_calls(near, far, poles, roots, vectors):
    children, rows, depth = vectors.shape
    cols = roots[0].shape[1]
    width = min(256, cols)
    tiles = cols // LANES
    chunk = rows // far
    block = chunk // near
    flops = 2 * children * chunk * depth * cols
    vectors = pltpu.with_memory_space_constraint(vectors, pltpu.HBM)
    *away, own_vec, panels = pl.pallas_call(
        functools.partial(away_kernel, near, far, width),
        out_shape=[pltpu.VMEM((children * tiles * (far - 1) * block + tail_rows(tiles), LANES), BF16)] * near
        + [pltpu.VMEM((children - 1, chunk, depth), BF16), pltpu.VMEM((children, cols, depth), BF16)],
        in_specs=[ANY] * 7,
        out_specs=[VMEM] * (near + 2),
        scratch_shapes=[
            pltpu.VMEM((children, rows - chunk, depth), BF16),
            pltpu.VMEM((children, 3, 8, depth), F32),
            pltpu.VMEM((2, children, depth), F32),
            pltpu.VMEM((2, children, depth), jnp.int32),
            pltpu.VMEM((1, cols), F32),
            pltpu.VMEM((1, cols), jnp.int32),
            pltpu.VMEM((2, cols, LANES), F32),
            pltpu.VMEM((cols, LANES), F32),
            pltpu.SemaphoreType.DMA((children, far)),
            pltpu.SemaphoreType.DMA((6,)),
        ],
        compiler_params=LARGE,
        cost_estimate=pl.CostEstimate(
            flops=flops * (far - 1),
            bytes_accessed=2 * children * rows * depth,
            transcendentals=children * depth * cols,
        ),
    )(*(pltpu.with_memory_space_constraint(x, pltpu.HBM) for x in (*poles, *roots)), vectors)
    own = pl.pallas_call(
        functools.partial(own_kernel, near, width),
        out_shape=[pltpu.VMEM((children * tiles * block, LANES), BF16)] * near,
        in_specs=[VMEM, VMEM, ANY],
        out_specs=[VMEM] * near,
        scratch_shapes=[pltpu.VMEM((chunk, depth), BF16), pltpu.SemaphoreType.DMA],
        compiler_params=LARGE,
        cost_estimate=pl.CostEstimate(flops=flops, bytes_accessed=0, transcendentals=0),
    )(own_vec, panels, vectors)
    return away, own


def middle_kernel(near, tiles, block, *refs):
    parts, total_ref, outs = refs[:near], refs[near + 1], refs[near + 2 :]
    total = read_tail(parts[0], tiles)
    for part in parts[1:]:
        total = total + read_tail(part, tiles)
    total_ref[...] = total
    groups = len(outs)
    rows = outs[0].shape[0] - tail_rows(tiles)
    size = rows if groups == 1 else block
    for group, out in enumerate(outs):
        write_tail(total, out)
        for first in range(0, rows, size):
            at = slice(first * groups + group * size, first * groups + (group + 1) * size)
            value = parts[0][at, :].astype(F32)
            for part in parts[1:]:
                value = value + part[at, :].astype(F32)
            out[first : first + size, :] = value.astype(BF16)


def middle_call(near, far, tiles, block, parts, after):
    rows = (parts[0].shape[0] - tail_rows(tiles)) // (far - 1)
    return pl.pallas_call(
        functools.partial(middle_kernel, near, tiles, block),
        out_shape=[jax.ShapeDtypeStruct((tiles, LANES), F32)]
        + [jax.ShapeDtypeStruct((rows + tail_rows(tiles), LANES), BF16)] * (far - 1),
        in_specs=[VMEM] * near + [ANY],
        out_specs=[VMEM] * far,
        compiler_params=SMALL,
    )(*parts, after)


def sum_kernel(*refs):
    value = refs[0][...].astype(F32)
    for part in refs[1:-1]:
        value = value + part[...].astype(F32)
    refs[-1][...] = value


def sum_call(parts):
    return pl.pallas_call(
        sum_kernel,
        out_shape=jax.ShapeDtypeStruct(parts[0].shape, F32),
        in_specs=[VMEM] * len(parts),
        out_specs=VMEM,
        compiler_params=SMALL,
        cost_estimate=pl.CostEstimate(flops=4 * 10**10, bytes_accessed=0, transcendentals=0),
    )(*parts)


def last_kernel(*refs):
    total_ref, own, others, out_ref = refs[0], refs[1], refs[2:-1], refs[-1]
    children, block, cols = out_ref.shape
    tiles = cols // LANES
    total = total_ref[...]
    for other in others:
        total = total + read_tail(other, tiles)
    scale = lax.rsqrt(total)
    for child in range(children):
        for tile in range(tiles):
            at = slice((child * tiles + tile) * block, (child * tiles + tile + 1) * block)
            value = own[at, :]
            for part in others:
                value = value + part[at, :].astype(F32)
            out_ref[child, :, tile * LANES : (tile + 1) * LANES] = (
                value * scale[tile : tile + 1, :]
            ).astype(BF16)


def exchange(parts, stride, n):
    got = list(parts)
    for k in sorted(range(1, len(parts)), key=lambda k: (k.bit_count(), -k)):
        got[k] = lax.ppermute(parts[k], "col", [(i, i ^ (k * stride)) for i in range(n)])
    return got


def solution(mesh):
    n = mesh.shape["col"]
    near, far = radices(n)

    def local(vectors, position, fraction, weight, retained, root_index, root_offset):
        children, rows, _ = vectors.shape
        cols = root_index.shape[0]
        block = rows // n
        roots = (root_index[None, :], root_offset[None, :])
        poles = (position, fraction, weight, retained)
        away, own = child_calls(near, far, poles, roots, vectors)
        away = exchange(away, 1, n)
        total, *sums = middle_call(near, far, cols // LANES, block, away, own[0])
        own = sum_call(exchange(own, 1, n))
        others = exchange([total] + sums, near, n)[1:]
        return pl.pallas_call(
            last_kernel,
            out_shape=jax.ShapeDtypeStruct((children, block, cols), BF16),
            in_specs=[VMEM] * (2 + len(others)),
            out_specs=VMEM,
            compiler_params=SMALL,
        )(total, own, *others)

    return jax.shard_map(
        local,
        mesh=mesh,
        in_specs=(P(None, "row", "col"),) + (P(None, "col"),) * 4 + (P(), P()),
        out_specs=P(None, ("row", "col"), None),
        check_vma=False,
    )
```

```python
import functools

import jax
import jax.numpy as jnp
from jax import lax
from jax.experimental import pallas as pl
from jax.experimental.pallas import tpu as pltpu
from jax.sharding import PartitionSpec as P

LANES = 128
VMEM = pl.BlockSpec(memory_space=pltpu.VMEM)
ANY = pl.BlockSpec(memory_space=pl.ANY)
F32, BF16 = jnp.float32, jnp.bfloat16
SMALL = pltpu.CompilerParams(vmem_limit_bytes=6 * 2**20)
LARGE = pltpu.CompilerParams(vmem_limit_bytes=24 * 2**20)


def radices(n):
    near = min(4, max(1, n // 2))
    return near, n // near


def tail_rows(tiles):
    return -(-3 * tiles // 16) * 16


def write_tail(total, ref):
    tiles = total.shape[0]
    high = total.astype(BF16).astype(F32)
    rest = total - high
    middle = rest.astype(BF16).astype(F32)
    pieces = [high, middle, rest - middle]
    spare = tail_rows(tiles) - 3 * tiles
    if spare:
        pieces.append(jnp.zeros((spare, LANES), F32))
    ref[ref.shape[0] - tail_rows(tiles) :, :] = jnp.concatenate(pieces, axis=0).astype(BF16)


def read_tail(ref, tiles):
    tail = ref[ref.shape[0] - tail_rows(tiles) :, :].astype(F32)
    return (tail[2 * tiles : 3 * tiles] + tail[tiles : 2 * tiles]) + tail[:tiles]


def multiply(vec, panel, first_tile, near, groups, outs):
    block = vec.shape[0] // (near * groups)
    me = lax.rem(lax.axis_index("col"), near)
    order = [(group, k) for group in range(groups) for k in range(near)]
    left = jnp.concatenate(
        [
            vec[pl.ds(pl.multiple_of((group * near + jnp.bitwise_xor(me, k)) * block, block), block), :]
            for group, k in order
        ],
        axis=0,
    )
    value = lax.dot_general(
        left, panel[...], (((1,), (1,)), ((), ())), preferred_element_type=F32
    ).astype(BF16)
    for place, (group, k) in enumerate(order):
        for tile in range(value.shape[1] // LANES):
            target = ((first_tile + tile) * groups + group) * block
            outs[k][target : target + block, :] = value[
                place * block : (place + 1) * block, tile * LANES : (tile + 1) * LANES
            ]


def away_kernel(near, far, width, *refs):
    pos_ref, frac_ref, weight_ref, kept_ref, root_ref, off_ref, vec_ref = refs[:7]
    outs = refs[7 : 7 + near]
    own_vec, panels, vec, poles, pole_in, kept_in, root_in, index_in, roots, sums, sems, in_sems = refs[7 + near :]
    children, cols, depth = panels.shape
    tiles = cols // LANES
    chunk = own_vec.shape[1]
    me = lax.div(lax.axis_index("col"), near)

    small = [
        pltpu.make_async_copy(source, target, in_sems.at[number])
        for number, (source, target) in enumerate(
            (
                (root_ref, index_in),
                (off_ref, root_in),
                (pos_ref, kept_in.at[0]),
                (frac_ref, pole_in.at[0]),
                (weight_ref, pole_in.at[1]),
                (kept_ref, kept_in.at[1]),
            )
        )
    ]
    large = [
        [
            pltpu.make_async_copy(
                vec_ref.at[child, pl.ds(pl.multiple_of(jnp.bitwise_xor(me, j) * chunk, chunk), chunk), :],
                vec.at[child, pl.ds((j - 1) * chunk, chunk), :] if j else own_vec.at[child],
                sems.at[child, j],
            )
            for j in range(1 if child + 1 == children else 0, far)
        ]
        for child in range(children)
    ]
    for copy in small:
        copy.start()
    for copies in large:
        for copy in copies[1 - far :]:
            copy.start()
    for copy in small[:2]:
        copy.wait()
    both = jnp.concatenate([index_in[...].astype(F32), root_in[...], jnp.zeros((6, cols), F32)], axis=0).T
    for copy in small[2:]:
        copy.wait()
    for copies in large[:-1]:
        copies[0].start()

    def prepare(child, first_col):
        if child == 0:
            here = slice(first_col, first_col + width)
            for number in range(2):
                roots[number, here, :] = jnp.broadcast_to(both[here, number : number + 1], (width, LANES))
        if first_col == 0:
            own = slice(child, child + 1)
            poles[child, 0] = jnp.broadcast_to(kept_in[0, own, :].astype(F32), (8, depth))
            poles[child, 1] = jnp.broadcast_to(pole_in[0, own, :], (8, depth))
            scaled = kept_in[1, own, :].astype(F32) * pole_in[1, own, :]
            poles[child, 2] = jnp.broadcast_to(scaled, (8, depth))

    def form(child, first_col):
        prepare(child, first_col)
        for row in range(first_col, first_col + width, 16):
            at = slice(row, row + 16)
            root = roots[0, at, :].reshape(2, 8, LANES)
            off = roots[1, at, :].reshape(2, 8, LANES)
            total = sums[at, :].reshape(2, 8, LANES) if child else jnp.zeros((2, 8, LANES), F32)
            for first in range(0, depth, LANES):
                here = slice(first, first + LANES)
                spacing = (poles[child, 0, :, here] - root) + (poles[child, 1, :, here] - off)
                raw = poles[child, 2, :, here] * pl.reciprocal(spacing, approx=True)
                total = total + raw * raw
                panels[child, at, here] = raw.reshape(16, LANES).astype(BF16)
            sums[at, :] = total.reshape(16, LANES)

    units = [(child, first) for child in range(children) for first in range(0, cols, width)]
    form(*units[0])
    for number, (child, first) in enumerate(units):
        if first == 0:
            for copy in large[child][1 - far :]:
                copy.wait()
        if number + 1 < len(units):
            form(*units[number + 1])
        else:
            total = jnp.concatenate(
                [
                    jnp.sum(sums[at : at + LANES, :].T, axis=0, keepdims=True)
                    for at in range(0, cols, LANES)
                ],
                axis=0,
            )
            for out in outs:
                write_tail(total, out)
        panel = panels.at[child, first : first + width, :]
        multiply(vec.at[child], panel, child * tiles + first // LANES, near, far - 1, outs)
    for copies in large[:-1]:
        copies[0].wait()


def own_kernel(near, width, own_vec, panels, vec_ref, *refs):
    outs, (last_vec, sem) = refs[:near], refs[near:]
    children, cols, _ = panels.shape
    chunk = last_vec.shape[0]
    me = lax.div(lax.axis_index("col"), near)
    rows = pl.ds(pl.multiple_of(me * chunk, chunk), chunk)
    copy = pltpu.make_async_copy(vec_ref.at[children - 1, rows, :], last_vec, sem)
    copy.start()
    for child in range(children):
        vec = last_vec if child + 1 == children else own_vec.at[child]
        if child + 1 == children:
            copy.wait()
        for first in range(0, cols, width):
            panel = panels.at[child, first : first + width, :]
            multiply(vec, panel, (child * cols + first) // LANES, near, 1, outs)


def child_calls(near, far, poles, roots, vectors):
    children, rows, depth = vectors.shape
    cols = roots[0].shape[1]
    width = min(256, cols)
    tiles = cols // LANES
    chunk = rows // far
    block = chunk // near
    flops = 2 * children * chunk * depth * cols
    vectors = pltpu.with_memory_space_constraint(vectors, pltpu.HBM)
    *away, own_vec, panels = pl.pallas_call(
        functools.partial(away_kernel, near, far, width),
        out_shape=[pltpu.VMEM((children * tiles * (far - 1) * block + tail_rows(tiles), LANES), BF16)] * near
        + [pltpu.VMEM((children - 1, chunk, depth), BF16), pltpu.VMEM((children, cols, depth), BF16)],
        in_specs=[ANY] * 7,
        out_specs=[VMEM] * (near + 2),
        scratch_shapes=[
            pltpu.VMEM((children, rows - chunk, depth), BF16),
            pltpu.VMEM((children, 3, 8, depth), F32),
            pltpu.VMEM((2, children, depth), F32),
            pltpu.VMEM((2, children, depth), jnp.int32),
            pltpu.VMEM((1, cols), F32),
            pltpu.VMEM((1, cols), jnp.int32),
            pltpu.VMEM((2, cols, LANES), F32),
            pltpu.VMEM((cols, LANES), F32),
            pltpu.SemaphoreType.DMA((children, far)),
            pltpu.SemaphoreType.DMA((6,)),
        ],
        compiler_params=LARGE,
        cost_estimate=pl.CostEstimate(
            flops=flops * (far - 1),
            bytes_accessed=2 * children * rows * depth,
            transcendentals=children * depth * cols,
        ),
    )(*(pltpu.with_memory_space_constraint(x, pltpu.HBM) for x in (*poles, *roots)), vectors)
    own = pl.pallas_call(
        functools.partial(own_kernel, near, width),
        out_shape=[pltpu.VMEM((children * tiles * block, LANES), BF16)] * near,
        in_specs=[VMEM, VMEM, ANY],
        out_specs=[VMEM] * near,
        scratch_shapes=[pltpu.VMEM((chunk, depth), BF16), pltpu.SemaphoreType.DMA],
        compiler_params=LARGE,
        cost_estimate=pl.CostEstimate(flops=flops, bytes_accessed=0, transcendentals=0),
    )(own_vec, panels, vectors)
    return away, own


def middle_kernel(near, tiles, block, *refs):
    parts, total_ref, outs = refs[:near], refs[near + 1], refs[near + 2 :]
    total = read_tail(parts[0], tiles)
    for part in parts[1:]:
        total = total + read_tail(part, tiles)
    total_ref[...] = total
    groups = len(outs)
    rows = outs[0].shape[0] - tail_rows(tiles)
    size = rows if groups == 1 else block
    for group, out in enumerate(outs):
        write_tail(total, out)
        for first in range(0, rows, size):
            at = slice(first * groups + group * size, first * groups + (group + 1) * size)
            value = parts[0][at, :].astype(F32)
            for part in parts[1:]:
                value = value + part[at, :].astype(F32)
            out[first : first + size, :] = value.astype(BF16)


def middle_call(near, far, tiles, block, parts, after):
    rows = (parts[0].shape[0] - tail_rows(tiles)) // (far - 1)
    return pl.pallas_call(
        functools.partial(middle_kernel, near, tiles, block),
        out_shape=[jax.ShapeDtypeStruct((tiles, LANES), F32)]
        + [jax.ShapeDtypeStruct((rows + tail_rows(tiles), LANES), BF16)] * (far - 1),
        in_specs=[VMEM] * near + [ANY],
        out_specs=[VMEM] * far,
        compiler_params=SMALL,
    )(*parts, after)


def sum_kernel(*refs):
    value = refs[0][...].astype(F32)
    for part in refs[1:-1]:
        value = value + part[...].astype(F32)
    refs[-1][...] = value


def sum_call(parts):
    return pl.pallas_call(
        sum_kernel,
        out_shape=jax.ShapeDtypeStruct(parts[0].shape, F32),
        in_specs=[VMEM] * len(parts),
        out_specs=VMEM,
        compiler_params=SMALL,
        cost_estimate=pl.CostEstimate(flops=4 * 10**10, bytes_accessed=0, transcendentals=0),
    )(*parts)


def last_kernel(*refs):
    total_ref, own, others, out_ref = refs[0], refs[1], refs[2:-1], refs[-1]
    children, block, cols = out_ref.shape
    tiles = cols // LANES
    total = total_ref[...]
    for other in others:
        total = total + read_tail(other, tiles)
    scale = lax.rsqrt(total)
    for child in range(children):
        for tile in range(tiles):
            at = slice((child * tiles + tile) * block, (child * tiles + tile + 1) * block)
            value = own[at, :]
            for part in others:
                value = value + part[at, :].astype(F32)
            out_ref[child, :, tile * LANES : (tile + 1) * LANES] = (
                value * scale[tile : tile + 1, :]
            ).astype(BF16)


def exchange(parts, stride, n):
    got = list(parts)
    for k in sorted(range(1, len(parts)), key=lambda k: (k.bit_count(), -k)):
        got[k] = lax.ppermute(parts[k], "col", [(i, i ^ (k * stride)) for i in range(n)])
    return got


def solution(mesh):
    n = mesh.shape["col"]
    near, far = radices(n)

    def local(vectors, position, fraction, weight, retained, root_index, root_offset):
        children, rows, _ = vectors.shape
        cols = root_index.shape[0]
        block = rows // n
        roots = (root_index[None, :], root_offset[None, :])
        poles = (position, fraction, weight, retained)
        away, own = child_calls(near, far, poles, roots, vectors)
        away = exchange(away, 1, n)
        total, *sums = middle_call(near, far, cols // LANES, block, away, own[0])
        own = sum_call(exchange(own, 1, n))
        others = exchange([total] + sums, near, n)[1:]
        return pl.pallas_call(
            last_kernel,
            out_shape=jax.ShapeDtypeStruct((children, block, cols), BF16),
            in_specs=[VMEM] * (2 + len(others)),
            out_specs=VMEM,
            compiler_params=SMALL,
        )(total, own, *others)

    return jax.shard_map(
        local,
        mesh=mesh,
        in_specs=(P(None, "row", "col"),) + (P(None, "col"),) * 4 + (P(), P()),
        out_specs=P(None, ("row", "col"), None),
        check_vma=False,
    )
```

```python
import functools

import jax
import jax.numpy as jnp
from jax import lax
from jax.experimental import pallas as pl
from jax.experimental.pallas import tpu as pltpu
from jax.sharding import PartitionSpec as P

LANES = 128
VMEM = pl.BlockSpec(memory_space=pltpu.VMEM)
ANY = pl.BlockSpec(memory_space=pl.ANY)
F32, BF16 = jnp.float32, jnp.bfloat16
SMALL = pltpu.CompilerParams(vmem_limit_bytes=6 * 2**20)
LARGE = pltpu.CompilerParams(vmem_limit_bytes=24 * 2**20)


def radices(n):
    near = min(4, max(1, n // 2))
    return near, n // near


def tail_rows(tiles):
    return -(-3 * tiles // 16) * 16


def write_tail(total, ref):
    tiles = total.shape[0]
    high = total.astype(BF16).astype(F32)
    rest = total - high
    middle = rest.astype(BF16).astype(F32)
    pieces = [high, middle, rest - middle]
    spare = tail_rows(tiles) - 3 * tiles
    if spare:
        pieces.append(jnp.zeros((spare, LANES), F32))
    ref[ref.shape[0] - tail_rows(tiles) :, :] = jnp.concatenate(pieces, axis=0).astype(BF16)


def read_tail(ref, tiles):
    tail = ref[ref.shape[0] - tail_rows(tiles) :, :].astype(F32)
    return (tail[2 * tiles : 3 * tiles] + tail[tiles : 2 * tiles]) + tail[:tiles]


def multiply(vec, panel, first_tile, near, groups, outs):
    block = vec.shape[0] // (near * groups)
    me = lax.rem(lax.axis_index("col"), near)
    order = [(group, k) for group in range(groups) for k in range(near)]
    left = jnp.concatenate(
        [
            vec[pl.ds(pl.multiple_of((group * near + jnp.bitwise_xor(me, k)) * block, block), block), :]
            for group, k in order
        ],
        axis=0,
    )
    value = lax.dot_general(
        left, panel[...], (((1,), (1,)), ((), ())), preferred_element_type=F32
    ).astype(BF16)
    for place, (group, k) in enumerate(order):
        for tile in range(value.shape[1] // LANES):
            target = ((first_tile + tile) * groups + group) * block
            outs[k][target : target + block, :] = value[
                place * block : (place + 1) * block, tile * LANES : (tile + 1) * LANES
            ]


def away_kernel(near, far, width, *refs):
    pos_ref, frac_ref, weight_ref, kept_ref, root_ref, off_ref, vec_ref = refs[:7]
    outs = refs[7 : 7 + near]
    own_vec, panels, vec, poles, pole_in, kept_in, root_in, index_in, roots, sums, sems, in_sems = refs[7 + near :]
    children, cols, depth = panels.shape
    tiles = cols // LANES
    chunk = own_vec.shape[1]
    me = lax.div(lax.axis_index("col"), near)

    small = [
        pltpu.make_async_copy(source, target, in_sems.at[number])
        for number, (source, target) in enumerate(
            (
                (root_ref, index_in),
                (off_ref, root_in),
                (pos_ref, kept_in.at[0]),
                (frac_ref, pole_in.at[0]),
                (weight_ref, pole_in.at[1]),
                (kept_ref, kept_in.at[1]),
            )
        )
    ]
    large = [
        [
            pltpu.make_async_copy(
                vec_ref.at[child, pl.ds(pl.multiple_of(jnp.bitwise_xor(me, j) * chunk, chunk), chunk), :],
                vec.at[child, pl.ds((j - 1) * chunk, chunk), :] if j else own_vec.at[child],
                sems.at[child, j],
            )
            for j in range(1 if child + 1 == children else 0, far)
        ]
        for child in range(children)
    ]
    for copy in small:
        copy.start()
    for copies in large:
        for copy in copies[1 - far :]:
            copy.start()
    for copy in small[:2]:
        copy.wait()
    both = jnp.concatenate([index_in[...].astype(F32), root_in[...], jnp.zeros((6, cols), F32)], axis=0).T
    for copy in small[2:]:
        copy.wait()
    for copies in large[:-1]:
        copies[0].start()

    def prepare(child, first_col):
        if child == 0:
            here = slice(first_col, first_col + width)
            for number in range(2):
                roots[number, here, :] = jnp.broadcast_to(both[here, number : number + 1], (width, LANES))
        if first_col == 0:
            own = slice(child, child + 1)
            poles[child, 0] = jnp.broadcast_to(kept_in[0, own, :].astype(F32), (8, depth))
            poles[child, 1] = jnp.broadcast_to(pole_in[0, own, :], (8, depth))
            scaled = kept_in[1, own, :].astype(F32) * pole_in[1, own, :]
            poles[child, 2] = jnp.broadcast_to(scaled, (8, depth))

    def form(child, first_col):
        prepare(child, first_col)
        for row in range(first_col, first_col + width, 16):
            at = slice(row, row + 16)
            root = roots[0, at, :].reshape(2, 8, LANES)
            off = roots[1, at, :].reshape(2, 8, LANES)
            total = sums[at, :].reshape(2, 8, LANES) if child else jnp.zeros((2, 8, LANES), F32)
            for first in range(0, depth, LANES):
                here = slice(first, first + LANES)
                spacing = (poles[child, 0, :, here] - root) + (poles[child, 1, :, here] - off)
                raw = poles[child, 2, :, here] * pl.reciprocal(spacing, approx=True)
                total = total + raw * raw
                panels[child, at, here] = raw.reshape(16, LANES).astype(BF16)
            sums[at, :] = total.reshape(16, LANES)

    units = [(child, first) for child in range(children) for first in range(0, cols, width)]
    form(*units[0])
    for number, (child, first) in enumerate(units):
        if first == 0:
            for copy in large[child][1 - far :]:
                copy.wait()
        if number + 1 < len(units):
            form(*units[number + 1])
        else:
            total = jnp.concatenate(
                [
                    jnp.sum(sums[at : at + LANES, :].T, axis=0, keepdims=True)
                    for at in range(0, cols, LANES)
                ],
                axis=0,
            )
            for out in outs:
                write_tail(total, out)
        panel = panels.at[child, first : first + width, :]
        multiply(vec.at[child], panel, child * tiles + first // LANES, near, far - 1, outs)
    for copies in large[:-1]:
        copies[0].wait()


def own_kernel(near, width, own_vec, panels, vec_ref, *refs):
    outs, (last_vec, sem) = refs[:near], refs[near:]
    children, cols, _ = panels.shape
    chunk = last_vec.shape[0]
    me = lax.div(lax.axis_index("col"), near)
    half = chunk // 2
    copies = [
        pltpu.make_async_copy(
            vec_ref.at[children - 1, pl.ds(pl.multiple_of(me * chunk + first, half), half), :],
            last_vec.at[first : first + half, :],
            sem.at[first // half],
        )
        for first in (0, half)
    ]
    for copy in copies:
        copy.start()
    for child in range(children):
        vec = last_vec if child + 1 == children else own_vec.at[child]
        if child + 1 == children:
            for copy in copies:
                copy.wait()
        for first in range(0, cols, width):
            panel = panels.at[child, first : first + width, :]
            multiply(vec, panel, (child * cols + first) // LANES, near, 1, outs)


def child_calls(near, far, poles, roots, vectors):
    children, rows, depth = vectors.shape
    cols = roots[0].shape[1]
    width = min(256, cols)
    tiles = cols // LANES
    chunk = rows // far
    block = chunk // near
    flops = 2 * children * chunk * depth * cols
    vectors = pltpu.with_memory_space_constraint(vectors, pltpu.HBM)
    *away, own_vec, panels = pl.pallas_call(
        functools.partial(away_kernel, near, far, width),
        out_shape=[pltpu.VMEM((children * tiles * (far - 1) * block + tail_rows(tiles), LANES), BF16)] * near
        + [pltpu.VMEM((children - 1, chunk, depth), BF16), pltpu.VMEM((children, cols, depth), BF16)],
        in_specs=[ANY] * 7,
        out_specs=[VMEM] * (near + 2),
        scratch_shapes=[
            pltpu.VMEM((children, rows - chunk, depth), BF16),
            pltpu.VMEM((children, 3, 8, depth), F32),
            pltpu.VMEM((2, children, depth), F32),
            pltpu.VMEM((2, children, depth), jnp.int32),
            pltpu.VMEM((1, cols), F32),
            pltpu.VMEM((1, cols), jnp.int32),
            pltpu.VMEM((2, cols, LANES), F32),
            pltpu.VMEM((cols, LANES), F32),
            pltpu.SemaphoreType.DMA((children, far)),
            pltpu.SemaphoreType.DMA((6,)),
        ],
        compiler_params=LARGE,
        cost_estimate=pl.CostEstimate(
            flops=flops * (far - 1),
            bytes_accessed=2 * children * rows * depth,
            transcendentals=children * depth * cols,
        ),
    )(*(pltpu.with_memory_space_constraint(x, pltpu.HBM) for x in (*poles, *roots)), vectors)
    own = pl.pallas_call(
        functools.partial(own_kernel, near, width),
        out_shape=[pltpu.VMEM((children * tiles * block, LANES), BF16)] * near,
        in_specs=[VMEM, VMEM, ANY],
        out_specs=[VMEM] * near,
        scratch_shapes=[pltpu.VMEM((chunk, depth), BF16), pltpu.SemaphoreType.DMA((2,))],
        compiler_params=LARGE,
        cost_estimate=pl.CostEstimate(flops=flops, bytes_accessed=0, transcendentals=0),
    )(own_vec, panels, vectors)
    return away, own


def middle_kernel(near, tiles, block, *refs):
    parts, total_ref, outs = refs[:near], refs[near + 1], refs[near + 2 :]
    total = read_tail(parts[0], tiles)
    for part in parts[1:]:
        total = total + read_tail(part, tiles)
    total_ref[...] = total
    groups = len(outs)
    rows = outs[0].shape[0] - tail_rows(tiles)
    size = rows if groups == 1 else block
    for group, out in enumerate(outs):
        write_tail(total, out)
        for first in range(0, rows, size):
            at = slice(first * groups + group * size, first * groups + (group + 1) * size)
            value = parts[0][at, :].astype(F32)
            for part in parts[1:]:
                value = value + part[at, :].astype(F32)
            out[first : first + size, :] = value.astype(BF16)


def middle_call(near, far, tiles, block, parts, after):
    rows = (parts[0].shape[0] - tail_rows(tiles)) // (far - 1)
    return pl.pallas_call(
        functools.partial(middle_kernel, near, tiles, block),
        out_shape=[jax.ShapeDtypeStruct((tiles, LANES), F32)]
        + [jax.ShapeDtypeStruct((rows + tail_rows(tiles), LANES), BF16)] * (far - 1),
        in_specs=[VMEM] * near + [ANY],
        out_specs=[VMEM] * far,
        compiler_params=SMALL,
    )(*parts, after)


def sum_kernel(*refs):
    value = refs[0][...].astype(F32)
    for part in refs[1:-1]:
        value = value + part[...].astype(F32)
    refs[-1][...] = value


def sum_call(parts):
    return pl.pallas_call(
        sum_kernel,
        out_shape=jax.ShapeDtypeStruct(parts[0].shape, F32),
        in_specs=[VMEM] * len(parts),
        out_specs=VMEM,
        compiler_params=SMALL,
        cost_estimate=pl.CostEstimate(flops=4 * 10**10, bytes_accessed=0, transcendentals=0),
    )(*parts)


def last_kernel(*refs):
    total_ref, own, others, out_ref = refs[0], refs[1], refs[2:-1], refs[-1]
    children, block, cols = out_ref.shape
    tiles = cols // LANES
    total = total_ref[...]
    for other in others:
        total = total + read_tail(other, tiles)
    scale = lax.rsqrt(total)
    for child in range(children):
        for tile in range(tiles):
            at = slice((child * tiles + tile) * block, (child * tiles + tile + 1) * block)
            value = own[at, :]
            for part in others:
                value = value + part[at, :].astype(F32)
            out_ref[child, :, tile * LANES : (tile + 1) * LANES] = (
                value * scale[tile : tile + 1, :]
            ).astype(BF16)


def exchange(parts, stride, n):
    got = list(parts)
    for k in sorted(range(1, len(parts)), key=lambda k: (k.bit_count(), -k)):
        got[k] = lax.ppermute(parts[k], "col", [(i, i ^ (k * stride)) for i in range(n)])
    return got


def solution(mesh):
    n = mesh.shape["col"]
    near, far = radices(n)

    def local(vectors, position, fraction, weight, retained, root_index, root_offset):
        children, rows, _ = vectors.shape
        cols = root_index.shape[0]
        block = rows // n
        roots = (root_index[None, :], root_offset[None, :])
        poles = (position, fraction, weight, retained)
        away, own = child_calls(near, far, poles, roots, vectors)
        away = exchange(away, 1, n)
        total, *sums = middle_call(near, far, cols // LANES, block, away, own[0])
        own = sum_call(exchange(own, 1, n))
        others = exchange([total] + sums, near, n)[1:]
        return pl.pallas_call(
            last_kernel,
            out_shape=jax.ShapeDtypeStruct((children, block, cols), BF16),
            in_specs=[VMEM] * (2 + len(others)),
            out_specs=VMEM,
            compiler_params=SMALL,
        )(total, own, *others)

    return jax.shard_map(
        local,
        mesh=mesh,
        in_specs=(P(None, "row", "col"),) + (P(None, "col"),) * 4 + (P(), P()),
        out_specs=P(None, ("row", "col"), None),
        check_vma=False,
    )
```

```python
import functools

import jax
import jax.numpy as jnp
from jax import lax
from jax.experimental import pallas as pl
from jax.experimental.pallas import tpu as pltpu
from jax.sharding import PartitionSpec as P

LANES = 128
VMEM = pl.BlockSpec(memory_space=pltpu.VMEM)
ANY = pl.BlockSpec(memory_space=pl.ANY)
F32, BF16 = jnp.float32, jnp.bfloat16
SMALL = pltpu.CompilerParams(vmem_limit_bytes=6 * 2**20)
LARGE = pltpu.CompilerParams(vmem_limit_bytes=24 * 2**20)


def radices(n):
    near = min(4, max(1, n // 2))
    return near, n // near


def tail_rows(tiles):
    return -(-3 * tiles // 16) * 16


def write_tail(total, ref):
    tiles = total.shape[0]
    high = total.astype(BF16).astype(F32)
    rest = total - high
    middle = rest.astype(BF16).astype(F32)
    pieces = [high, middle, rest - middle]
    spare = tail_rows(tiles) - 3 * tiles
    if spare:
        pieces.append(jnp.zeros((spare, LANES), F32))
    ref[ref.shape[0] - tail_rows(tiles) :, :] = jnp.concatenate(pieces, axis=0).astype(BF16)


def read_tail(ref, tiles):
    tail = ref[ref.shape[0] - tail_rows(tiles) :, :].astype(F32)
    return (tail[2 * tiles : 3 * tiles] + tail[tiles : 2 * tiles]) + tail[:tiles]


def multiply(vec, panel, first_tile, near, groups, outs):
    block = vec.shape[0] // (near * groups)
    me = lax.rem(lax.axis_index("col"), near)
    order = [(group, k) for group in range(groups) for k in range(near)]
    left = jnp.concatenate(
        [
            vec[pl.ds(pl.multiple_of((group * near + jnp.bitwise_xor(me, k)) * block, block), block), :]
            for group, k in order
        ],
        axis=0,
    )
    value = lax.dot_general(
        left, panel[...], (((1,), (1,)), ((), ())), preferred_element_type=F32
    ).astype(BF16)
    for place, (group, k) in enumerate(order):
        for tile in range(value.shape[1] // LANES):
            target = ((first_tile + tile) * groups + group) * block
            outs[k][target : target + block, :] = value[
                place * block : (place + 1) * block, tile * LANES : (tile + 1) * LANES
            ]


def away_kernel(near, far, width, *refs):
    pos_ref, frac_ref, weight_ref, kept_ref, root_ref, off_ref, vec_ref = refs[:7]
    outs = refs[7 : 7 + near]
    own_vec, panels, vec, poles, pole_in, kept_in, root_in, index_in, roots, sums, sems, in_sems = refs[7 + near :]
    children, cols, depth = panels.shape
    tiles = cols // LANES
    chunk = own_vec.shape[1]
    me = lax.div(lax.axis_index("col"), near)

    small = [
        pltpu.make_async_copy(source, target, in_sems.at[number])
        for number, (source, target) in enumerate(
            (
                (root_ref, index_in),
                (off_ref, root_in),
                (pos_ref, kept_in.at[0]),
                (frac_ref, pole_in.at[0]),
                (weight_ref, pole_in.at[1]),
                (kept_ref, kept_in.at[1]),
            )
        )
    ]
    large = [
        [
            pltpu.make_async_copy(
                vec_ref.at[child, pl.ds(pl.multiple_of(jnp.bitwise_xor(me, j) * chunk, chunk), chunk), :],
                vec.at[child, pl.ds((j - 1) * chunk, chunk), :] if j else own_vec.at[child],
                sems.at[child, j],
            )
            for j in range(1 if child + 1 == children else 0, far)
        ]
        for child in range(children)
    ]
    for copy in small:
        copy.start()
    for copies in large:
        for copy in copies[1 - far :]:
            copy.start()
    for copy in small[:2]:
        copy.wait()
    both = jnp.concatenate([index_in[...].astype(F32), root_in[...], jnp.zeros((6, cols), F32)], axis=0).T
    for copy in small[2:]:
        copy.wait()
    for copies in large[:-1]:
        copies[0].start()

    def prepare(child, first_col):
        if child == 0:
            here = slice(first_col, first_col + width)
            for number in range(2):
                roots[number, here, :] = jnp.broadcast_to(both[here, number : number + 1], (width, LANES))
        if first_col == 0:
            own = slice(child, child + 1)
            poles[child, 0] = jnp.broadcast_to(kept_in[0, own, :].astype(F32), (8, depth))
            poles[child, 1] = jnp.broadcast_to(pole_in[0, own, :], (8, depth))
            scaled = kept_in[1, own, :].astype(F32) * pole_in[1, own, :]
            poles[child, 2] = jnp.broadcast_to(scaled, (8, depth))

    def form(child, first_col):
        prepare(child, first_col)
        for row in range(first_col, first_col + width, 16):
            at = slice(row, row + 16)
            root = roots[0, at, :].reshape(2, 8, LANES)
            off = roots[1, at, :].reshape(2, 8, LANES)
            total = sums[at, :].reshape(2, 8, LANES) if child else jnp.zeros((2, 8, LANES), F32)
            for first in range(0, depth, LANES):
                here = slice(first, first + LANES)
                spacing = (poles[child, 0, :, here] - root) + (poles[child, 1, :, here] - off)
                raw = poles[child, 2, :, here] * pl.reciprocal(spacing, approx=True)
                total = total + raw * raw
                panels[child, at, here] = raw.reshape(16, LANES).astype(BF16)
            sums[at, :] = total.reshape(16, LANES)

    units = [(child, first) for child in range(children) for first in range(0, cols, width)]
    form(*units[0])
    for number, (child, first) in enumerate(units):
        if first == 0:
            for copy in large[child][1 - far :]:
                copy.wait()
        if number + 1 < len(units):
            form(*units[number + 1])
        else:
            total = jnp.concatenate(
                [
                    jnp.sum(sums[at : at + LANES, :].T, axis=0, keepdims=True)
                    for at in range(0, cols, LANES)
                ],
                axis=0,
            )
            for out in outs:
                write_tail(total, out)
        panel = panels.at[child, first : first + width, :]
        multiply(vec.at[child], panel, child * tiles + first // LANES, near, far - 1, outs)
    for copies in large[:-1]:
        copies[0].wait()


def own_kernel(near, width, own_vec, panels, vec_ref, *refs):
    outs, (last_vec, sem) = refs[:near], refs[near:]
    children, cols, _ = panels.shape
    chunk = last_vec.shape[0]
    me = lax.div(lax.axis_index("col"), near)
    rows = pl.ds(pl.multiple_of(me * chunk, chunk), chunk)
    copy = pltpu.make_async_copy(vec_ref.at[children - 1, rows, :], last_vec, sem)
    copy.start()
    for child in range(children):
        vec = last_vec if child + 1 == children else own_vec.at[child]
        if child + 1 == children:
            copy.wait()
        for first in range(0, cols, width):
            panel = panels.at[child, first : first + width, :]
            multiply(vec, panel, (child * cols + first) // LANES, near, 1, outs)


def child_calls(near, far, poles, roots, vectors):
    children, rows, depth = vectors.shape
    cols = roots[0].shape[1]
    width = min(256, cols)
    tiles = cols // LANES
    chunk = rows // far
    block = chunk // near
    flops = 2 * children * chunk * depth * cols
    vectors = pltpu.with_memory_space_constraint(vectors, pltpu.HBM)
    *away, own_vec, panels = pl.pallas_call(
        functools.partial(away_kernel, near, far, width),
        out_shape=[pltpu.VMEM((children * tiles * (far - 1) * block + tail_rows(tiles), LANES), BF16)] * near
        + [pltpu.VMEM((children - 1, chunk, depth), BF16), pltpu.VMEM((children, cols, depth), BF16)],
        in_specs=[ANY] * 7,
        out_specs=[VMEM] * (near + 2),
        scratch_shapes=[
            pltpu.VMEM((children, rows - chunk, depth), BF16),
            pltpu.VMEM((children, 3, 8, depth), F32),
            pltpu.VMEM((2, children, depth), F32),
            pltpu.VMEM((2, children, depth), jnp.int32),
            pltpu.VMEM((1, cols), F32),
            pltpu.VMEM((1, cols), jnp.int32),
            pltpu.VMEM((2, cols, LANES), F32),
            pltpu.VMEM((cols, LANES), F32),
            pltpu.SemaphoreType.DMA((children, far)),
            pltpu.SemaphoreType.DMA((6,)),
        ],
        compiler_params=LARGE,
        cost_estimate=pl.CostEstimate(
            flops=flops * (far - 1),
            bytes_accessed=2 * children * rows * depth,
            transcendentals=children * depth * cols,
        ),
    )(*(pltpu.with_memory_space_constraint(x, pltpu.HBM) for x in (*poles, *roots)), vectors)
    own = pl.pallas_call(
        functools.partial(own_kernel, near, width),
        out_shape=[pltpu.VMEM((children * tiles * block, LANES), BF16)] * near,
        in_specs=[VMEM, VMEM, ANY],
        out_specs=[VMEM] * near,
        scratch_shapes=[pltpu.VMEM((chunk, depth), BF16), pltpu.SemaphoreType.DMA],
        compiler_params=LARGE,
        cost_estimate=pl.CostEstimate(flops=flops, bytes_accessed=0, transcendentals=0),
    )(own_vec, panels, vectors)
    return away, own


def middle_kernel(near, tiles, block, *refs):
    parts, total_ref, outs = refs[:near], refs[near + 1], refs[near + 2 :]
    total = read_tail(parts[0], tiles)
    for part in parts[1:]:
        total = total + read_tail(part, tiles)
    total_ref[...] = total
    groups = len(outs)
    rows = outs[0].shape[0] - tail_rows(tiles)
    size = rows if groups == 1 else block
    for group, out in enumerate(outs):
        write_tail(total, out)
        for first in range(0, rows, size):
            at = slice(first * groups + group * size, first * groups + (group + 1) * size)
            value = parts[0][at, :].astype(F32)
            for part in parts[1:]:
                value = value + part[at, :].astype(F32)
            out[first : first + size, :] = value.astype(BF16)


def middle_call(near, far, tiles, block, parts, after):
    rows = (parts[0].shape[0] - tail_rows(tiles)) // (far - 1)
    return pl.pallas_call(
        functools.partial(middle_kernel, near, tiles, block),
        out_shape=[jax.ShapeDtypeStruct((tiles, LANES), F32)]
        + [jax.ShapeDtypeStruct((rows + tail_rows(tiles), LANES), BF16)] * (far - 1),
        in_specs=[VMEM] * near + [ANY],
        out_specs=[VMEM] * far,
        compiler_params=SMALL,
    )(*parts, after)


def sum_kernel(*refs):
    value = refs[0][...].astype(F32)
    for part in refs[1:-1]:
        value = value + part[...].astype(F32)
    refs[-1][...] = value


def sum_call(parts):
    return pl.pallas_call(
        sum_kernel,
        out_shape=jax.ShapeDtypeStruct(parts[0].shape, F32),
        in_specs=[VMEM] * len(parts),
        out_specs=VMEM,
        compiler_params=SMALL,
        cost_estimate=pl.CostEstimate(flops=4 * 10**10, bytes_accessed=0, transcendentals=0),
    )(*parts)


def last_kernel(*refs):
    total_ref, own, others, (out_ref, held, sems) = refs[0], refs[1], refs[2:-3], refs[-3:]
    children, block, cols = held.shape
    copies = [pltpu.make_async_copy(held.at[child], out_ref.at[child], sems.at[child]) for child in range(children)]
    tiles = cols // LANES
    total = total_ref[...]
    for other in others:
        total = total + read_tail(other, tiles)
    scale = lax.rsqrt(total)
    for child in range(children):
        for tile in range(tiles):
            at = slice((child * tiles + tile) * block, (child * tiles + tile + 1) * block)
            value = own[at, :]
            for part in others:
                value = value + part[at, :].astype(F32)
            held[child, :, tile * LANES : (tile + 1) * LANES] = (
                value * scale[tile : tile + 1, :]
            ).astype(BF16)
        copies[child].start()
    for copy in copies:
        copy.wait()


def exchange(parts, stride, n):
    got = list(parts)
    for k in sorted(range(1, len(parts)), key=lambda k: (k.bit_count(), -k)):
        got[k] = lax.ppermute(parts[k], "col", [(i, i ^ (k * stride)) for i in range(n)])
    return got


def solution(mesh):
    n = mesh.shape["col"]
    near, far = radices(n)

    def local(vectors, position, fraction, weight, retained, root_index, root_offset):
        children, rows, _ = vectors.shape
        cols = root_index.shape[0]
        block = rows // n
        roots = (root_index[None, :], root_offset[None, :])
        poles = (position, fraction, weight, retained)
        away, own = child_calls(near, far, poles, roots, vectors)
        away = exchange(away, 1, n)
        total, *sums = middle_call(near, far, cols // LANES, block, away, own[0])
        own = sum_call(exchange(own, 1, n))
        others = exchange([total] + sums, near, n)[1:]
        return pl.pallas_call(
            last_kernel,
            out_shape=jax.ShapeDtypeStruct((children, block, cols), BF16),
            in_specs=[VMEM] * (2 + len(others)),
            out_specs=ANY,
            scratch_shapes=[pltpu.VMEM((children, block, cols), BF16), pltpu.SemaphoreType.DMA((children,))],
            compiler_params=SMALL,
        )(total, own, *others)

    return jax.shard_map(
        local,
        mesh=mesh,
        in_specs=(P(None, "row", "col"),) + (P(None, "col"),) * 4 + (P(), P()),
        out_specs=P(None, ("row", "col"), None),
        check_vma=False,
    )
```
